32 devices in a mesh: groups: 2 (over y), tensor: 4 (over z), section: 2 (over x), seq: 2 (over core).
Axes of the slice: x: 2, y: 2, z: 4, core: 2. Of those that a mesh axis runs over, the one named last changes fastest.
Arguments:
- token_ids: int32 [4, 96], P('groups'), parts along dimension 0, may hold values from 0 to 511
- leading_span_index: int32 [2], P('groups'), parts along dimension 0, may hold values from 8 to 4103
- embed_table: float32 [512, 8192], P(None, 'tensor'), may hold values from -6 to 6
- norm_gain: float32 [2, 8192], P('section', 'tensor'), may hold values from 0.25 to 1.75
- decay_rates: float32 [2, 16, 8192], P('section', None, 'tensor'), may hold values from 0.0002 to 0.03
- residues: float32 [2, 16, 8192], P('section', None, 'tensor'), may hold values from -0.12 to 0.12
- history: float32 [2, 8, 192, 8192], P('section', 'seq', 'groups', 'tensor'), parts along dimension 2, may hold values from -6 to 6
- mix_weight: bfloat16 [2, 8192, 8192], P('section', None, ('tensor', 'seq')), may hold values from -0.0625 to 0.0625
Outputs:
- section_out: float32 [2, 2, 192, 8192], P('section', None, 'groups', ('tensor', 'seq')), parts along dimension 2
The draws below stay inside these ranges and needn't reach their ends.
There are 2 independent parts, one for each index of `groups`. The reference program is written for one: setup_inputs(seed, part) draws one part's arguments, and reference() takes and returns one part's arrays. A program takes and returns all parts, laid end to end along the dimension named above; an argument that names none is the same for every part. Nothing has to cross between parts.
Inputs may be any that keep to these rules, and one draw needn't show every extreme that they name: `leading_span_index`: index of the first span of the run; the span before it is the newest one in history.
All inputs are finite; a program needn't handle non-finite values.
Results may differ from the reference program's by a relative error of at most 0.0036.
Values may be sent and summed in bfloat16 or wider, within the bound.
A program may use at most 128 MiB of HBM per device.

```python
import math
import jax
import jax.numpy as jnp
from jax import lax

MODEL_WIDTH = 8192
VOCAB = 512
MODES = 16
SPANS = 2
SPAN_TOKENS = 96
HISTORY_SPANS = 8
SECTION_LAYERS = 2


def place_ends(array, stream_key, low, top_value):
    spot = [jax.random.randint(jax.random.fold_in(stream_key, axis), (), 0, length) for axis, length in enumerate(array.shape)]
    widest = array.shape.index(max(array.shape))
    beside = spot[:widest] + [(spot[widest] + 1) % array.shape[widest]] + spot[widest + 1:]
    return array.at[tuple(spot)].set(low).at[tuple(beside)].set(top_value)


def shard_levels(key, extent, cuts, low, high):
    level = 1.0
    for axis_at, parts in cuts:
        steps = jax.random.uniform(jax.random.fold_in(jax.random.fold_in(key, 6), axis_at), (parts,), jnp.float32, low / len(cuts), high / len(cuts))
        level = level * jnp.repeat(jnp.exp(steps), extent[axis_at] // parts).reshape((-1,) + (1,) * (len(extent) - 1 - axis_at))
    return level


def noise(key, shape, deviation, bound, shards=(), dtype=jnp.bfloat16):
    entries = jax.random.normal(key, shape, jnp.float32) * deviation
    if len(shards) > 0:
        entries = shard_levels(key, shape, shards, -0.22, 0.18) * entries
    return jnp.clip(entries, min=-bound, max=bound).astype(dtype)


def setup_inputs(seed: int = 0, part: int = 0) -> dict:
    arg_keys = jax.random.split(jax.random.key(seed), 9)
    own_keys = jax.random.split(jax.random.fold_in(arg_keys[8], part), 9)
    token_ids = place_ends(jax.random.randint(own_keys[0], (SPANS, SPAN_TOKENS), 0, VOCAB), jax.random.fold_in(own_keys[0], 1), 0, VOCAB - 1).astype(jnp.int32)
    leading_span_index = jax.random.randint(own_keys[1], (1,), HISTORY_SPANS, HISTORY_SPANS + 4096).astype(jnp.int32)
    embed_table = noise(arg_keys[2], (VOCAB, MODEL_WIDTH), 1.0, 6.0, ((1, 4),), jnp.float32)
    norm_gain = jnp.clip(1.0 + 0.15 * jax.random.normal(arg_keys[3], (SECTION_LAYERS, MODEL_WIDTH), jnp.float32), 0.25, 1.75)
    decay_rates = jnp.clip(jnp.exp(math.log(0.03) - 5.0106353 * jax.random.uniform(arg_keys[4], (SECTION_LAYERS, MODES, MODEL_WIDTH), jnp.float32) ** shard_levels(arg_keys[4], (SECTION_LAYERS, MODES, MODEL_WIDTH), ((0, 2), (2, 4)), -0.2, 0.2)), 0.0002, 0.03)
    residues = noise(arg_keys[5], (SECTION_LAYERS, MODES, MODEL_WIDTH), 0.02, 0.12, ((0, 2), (2, 4)), jnp.float32)
    history = noise(own_keys[6], (SECTION_LAYERS, HISTORY_SPANS, SPAN_TOKENS, MODEL_WIDTH), 1.0, 6.0, ((0, 2), (1, 2), (3, 4)), jnp.float32)
    mix_weight = noise(arg_keys[7], (SECTION_LAYERS, MODEL_WIDTH, MODEL_WIDTH), MODEL_WIDTH ** -0.5, 0.0625, ((0, 2), (2, 8)))
    return dict(token_ids=token_ids, leading_span_index=leading_span_index, embed_table=embed_table, norm_gain=norm_gain, decay_rates=decay_rates, residues=residues, history=history, mix_weight=mix_weight)


def build_taps(rates, weights, count):
    lag_pos = jnp.arange(count).astype(jnp.float32)
    taps_sum = jnp.zeros((count, rates.shape[1]), jnp.float32)
    for mode_num in range(rates.shape[0]):
        taps_sum = taps_sum + weights[mode_num][None, :] * jnp.exp(-rates[mode_num][None, :] * lag_pos[:, None])
    return taps_sum

def causal_conv(signal, taps_all):
    count = signal.shape[0]
    length = 2 * count
    spectrum = jnp.fft.rfft(signal, n=length, axis=0) * jnp.fft.rfft(taps_all, n=length, axis=0)
    return jnp.fft.irfft(spectrum, n=length, axis=0)[:count].astype(jnp.float32)

def reference(token_ids, leading_span_index, embed_table, norm_gain, decay_rates, residues, history, mix_weight):
    slot_total = history.shape[1]
    row_count = token_ids.shape[1]
    width = embed_table.shape[1]
    first_span = leading_span_index[0]
    slot_ages = jnp.arange(slot_total, 0, -1).astype(jnp.int32)
    slot_order = ((first_span - slot_ages) % slot_total).astype(jnp.int32)
    current = jnp.take(embed_table, token_ids, axis=0)
    results = []
    for section_num in range(SECTION_LAYERS):
        mean_sq = lax.optimization_barrier(jnp.mean(current * current, axis=-1))
        normed = current * lax.rsqrt(mean_sq + 1e-05)[..., None] * norm_gain[section_num][None, None, :]
        past = jnp.take(history[section_num], slot_order, axis=0).reshape(slot_total * row_count, width)
        sequence_a = jnp.concatenate([past, normed[0]], axis=0)
        sequence_b = jnp.concatenate([past[row_count:], normed[0], normed[1]], axis=0)
        count = sequence_a.shape[0]
        taps_all = build_taps(decay_rates[section_num], residues[section_num], count)
        conv_a = causal_conv(sequence_a, taps_all)[count - row_count:]
        conv_b = causal_conv(sequence_b, taps_all)[count - row_count:]
        conv_out = jnp.stack([conv_a, conv_b])
        gated = (normed * conv_out).astype(jnp.bfloat16)
        mixed = jnp.dot(gated.reshape(-1, width), mix_weight[section_num], preferred_element_type=jnp.float32)
        current = current + mixed.reshape(current.shape)
        results.append(current)
    return jnp.stack(results)
```

```python
import functools

import jax
import jax.numpy as jnp
from jax import lax
from jax.experimental import pallas as pl
from jax.experimental.pallas import tpu as pltpu
from jax.sharding import PartitionSpec as P

epsilon = 1e-05
LANES = 128
MESH = pl.DeviceIdType.MESH


def spread(start, count, stride):
    return pl.ds(start, count, stride=stride) if count > 1 else pl.ds(start, 1)


def kernel(
    dims,
    ids_ref,
    lead_ref,
    gain_ref,
    embed_hbm,
    rates_hbm,
    residues_hbm,
    history_hbm,
    weight_hbm,
    out_ref,
    embed,
    rates,
    residues,
    history,
    weight,
    decay,
    part_send,
    part_recv,
    part_own,
    state_keep,
    x_ref,
    normed,
    conv,
    total,
    squares,
    gathered,
    x_send,
    x_recv,
    load_sem,
    part_sem,
    sq_send,
    sq_recv,
    z_send,
    z_recv,
    f_send,
    f_recv,
    s_send,
    s_recv,
):
    spans, rows, half, width, modes, slots, vocab, tensor_n, section_n, seq_n = dims
    chunks = half // LANES
    padded = (rows + LANES - 1) // LANES * LANES
    t = lax.axis_index("tensor")
    s = lax.axis_index("section")
    q = lax.axis_index("seq")
    partner = 1 - q
    me = t * seq_n + q
    peers = tensor_n * seq_n
    model_width = half * peers
    direction = 1 - 2 * ((2 * t) // tensor_n)
    first_section = s == 0
    has_next = s + 1 < section_n

    def at_tensor(step):
        return lax.rem(t + direction * step + tensor_n, tensor_n)

    def loads(with_embed):
        found = []
        for j in range(width // LANES):
            lanes = pl.ds(j * LANES, LANES)
            found.append((rates_hbm.at[0, :, lanes], rates.at[pl.ds(j * modes, modes), :], 0))
            found.append((residues_hbm.at[0, :, lanes], residues.at[pl.ds(j * modes, modes), :], 1))
            for i in range(slots):
                found.append((history_hbm.at[0, i, :, lanes], history.at[i, pl.ds(j * rows, rows), :], 2))
        return found

    barrier = pltpu.get_barrier_semaphore()

    def greet(step, carry):
        other = lax.rem(me + step, peers)
        pl.semaphore_signal(
            barrier, inc=1, device_id={"tensor": other // seq_n, "seq": other % seq_n}, device_id_type=MESH
        )
        return carry

    @pl.when(first_section)
    def _():
        for j in range(chunks):
            lanes = pl.ds(pl.multiple_of(q * half + j * LANES, LANES), LANES)
            pltpu.make_async_copy(embed_hbm.at[:, lanes], embed.at[pl.ds(j * vocab, vocab), :], load_sem.at[3]).start()

    for source, target, which in loads(False):
        pltpu.make_async_copy(source, target, load_sem.at[which]).start()
    weight_copy = pltpu.make_async_copy(weight_hbm.at[0], weight, load_sem.at[4])
    weight_copy.start()

    lax.fori_loop(1, peers, greet, 0)

    @pl.when(has_next)
    def _():
        pl.semaphore_signal(barrier, inc=1, device_id={"section": s + 1}, device_id_type=MESH)

    @pl.when(s > 0)
    def _():
        pl.semaphore_signal(barrier, inc=1, device_id={"section": s - 1}, device_id_type=MESH)

    neighbours = jnp.where(has_next, 1, 0) + jnp.where(s > 0, 1, 0)
    pl.semaphore_wait(barrier, peers - 1 + neighbours)

    def square_copy(c, source, step, send_to):
        other = lax.rem(me + step, peers)
        slot = me if send_to else other
        return pltpu.make_async_remote_copy(
            src_ref=squares.at[c, slot],
            dst_ref=squares.at[c, slot],
            send_sem=sq_send.at[c, step],
            recv_sem=sq_recv.at[c, slot],
            device_id={"tensor": other // seq_n, "seq": other % seq_n},
            device_id_type=MESH,
        )

    def share_squares(c):
        acc = jnp.zeros((rows, LANES), jnp.float32)
        for j in range(chunks):
            piece = x_ref[c, pl.ds(j * rows, rows), :]
            acc = acc + piece * piece
        if padded > rows:
            acc = jnp.concatenate([acc, jnp.zeros((padded - rows, LANES), jnp.float32)], axis=0)
        by_row = jnp.sum(acc.T, axis=0, keepdims=True)
        squares[c, me] = jnp.broadcast_to(by_row, (8, padded))

        def send(step, carry):
            square_copy(c, me, step, True).start()
            return carry

        lax.fori_loop(1, peers, send, 0)

    def embed_rows(c):
        def one(p, carry):
            x_ref[c, spread(p, chunks, rows), :] = embed[spread(ids_ref[c, p], chunks, vocab), :]
            return carry

        lax.fori_loop(0, rows, one, 0, unroll=8)
        share_squares(c)

    def arrive_rows(c):
        pltpu.make_async_remote_copy(
            src_ref=x_send.at[c],
            dst_ref=x_recv.at[c],
            send_sem=s_send.at[c],
            recv_sem=s_recv.at[c],
            device_id={"section": s - 1},
            device_id_type=MESH,
        ).wait_recv()
        for j in range(chunks):
            block = pl.ds(j * rows, rows)
            x_ref[c, block, :] = x_recv[c, block, :].astype(jnp.float32)
        share_squares(c)

    def z_copy(c, step, send_to):
        other = at_tensor(step)
        slot = me if send_to else other * seq_n + q
        return pltpu.make_async_remote_copy(
            src_ref=gathered.at[c, slot],
            dst_ref=gathered.at[c, slot],
            send_sem=z_send.at[c, other],
            recv_sem=z_recv.at[c, t if send_to else other],
            device_id={"tensor": other},
            device_id_type=MESH,
        )

    def f_copy(c, step, send_to):
        other = at_tensor(step)
        slot = other * seq_n + (q if send_to else partner)
        return pltpu.make_async_remote_copy(
            src_ref=gathered.at[c, slot],
            dst_ref=gathered.at[c, slot],
            send_sem=f_send.at[c, other],
            recv_sem=f_recv.at[c, other],
            device_id={"seq": partner},
            device_id_type=MESH,
        )

    def start_sends(c):
        f_copy(c, 0, True).start()

        def send(step, carry):
            z_copy(c, step, True).start()
            return carry

        lax.fori_loop(1, tensor_n, send, 0)

    def make_gated(c):
        def wait(step, carry):
            square_copy(c, me, step, False).wait_recv()
            return carry

        lax.fori_loop(1, peers, wait, 0)
        summed = jnp.sum(squares[c], axis=0)
        scale = lax.rsqrt(summed * (1.0 / model_width) + epsilon)
        scale = jnp.broadcast_to(scale[0:1, :], (LANES, padded)).T[:rows]
        for j in range(chunks):
            block = pl.ds(j * rows, rows)
            gain = gain_ref[0:1, pl.ds(pl.multiple_of(q * half + j * LANES, LANES), LANES)]
            normed[c, block, :] = x_ref[c, block, :] * (scale * gain)

        decays = decay[...]
        gains = jnp.stack([residues[spread(q * chunks * modes + m, chunks, modes), :] for m in range(modes)])

        def step(p, state):
            row = normed[c, spread(p, chunks, rows), :]
            state = state * decays + gains * row[None]
            conv[c, spread(p, chunks, rows), :] = jnp.sum(state, axis=0)
            return state

        state = lax.fori_loop(0, rows, step, state_keep[0], unroll=4)
        state_keep[0] = state - state_keep[1]
        for j in range(chunks):
            block = pl.ds(j * rows, rows)
            gathered[c, me, :, pl.ds(j * LANES, LANES)] = (normed[c, block, :] * conv[c, block, :]).astype(
                jnp.bfloat16
            )

    def multiply(c, slot):
        block = weight[pl.ds(pl.multiple_of(slot * half, half), half), :]
        total[...] += jnp.dot(gathered[c, slot], block, preferred_element_type=jnp.float32)

    def project(c):
        total[...] = jnp.zeros_like(total)
        multiply(c, me)

        def take(step, carry):
            z_copy(c, step, False).wait_recv()
            f_copy(c, step, True).start()
            multiply(c, at_tensor(step) * seq_n + q)
            f_copy(c, step - 1, False).wait_recv()
            multiply(c, at_tensor(step - 1) * seq_n + partner)
            return carry

        lax.fori_loop(1, tensor_n, take, 0)

    def finish(c):
        f_copy(c, tensor_n - 1, False).wait_recv()
        multiply(c, at_tensor(tensor_n - 1) * seq_n + partner)
        for j in range(chunks):
            lanes = pl.ds(j * LANES, LANES)
            block = pl.ds(j * rows, rows)
            value = x_ref[c, block, :] + total[:, lanes]
            out_ref[0, c, :, lanes] = value
            x_send[c, block, :] = value.astype(jnp.bfloat16)

        @pl.when(has_next)
        def _():
            section_copy(c).start()

    def section_copy(c):
        return pltpu.make_async_remote_copy(
            src_ref=x_send.at[c],
            dst_ref=x_recv.at[c],
            send_sem=s_send.at[c],
            recv_sem=s_recv.at[c],
            device_id={"section": s + 1},
            device_id_type=MESH,
        )

    @pl.when(first_section)
    def _():
        pltpu.make_async_copy(embed, embed, load_sem.at[3]).wait()
        for c in range(spans):
            embed_rows(c)

    pltpu.make_async_copy(rates, rates, load_sem.at[0]).wait()
    pltpu.make_async_copy(residues, residues, load_sem.at[1]).wait()
    pltpu.make_async_copy(history, history, load_sem.at[2]).wait()
    first_span = lead_ref[0]
    slot_total = slots * seq_n

    def history_part(side, target):
        rate = jnp.stack([rates[spread(side * chunks * modes + m, chunks, modes), :] for m in range(modes)])
        decay[...] = jnp.exp(-rate)
        target[...] = jnp.zeros_like(target)

        def one_slot(i, carry):
            decays = decay[...]

            def step(l, state):
                row = history[i, spread(side * chunks * rows + l, chunks, rows), :]
                return state * decays + row[None]

            state = lax.fori_loop(0, rows, step, jnp.zeros((modes, chunks, LANES), jnp.float32), unroll=8)
            age = lax.rem(first_span - 1 - (q * slots + i), slot_total) + 1
            back = ((age - 1) * rows).astype(jnp.float32)
            oldest = jnp.where(age == slot_total, 1.0, 0.0).astype(jnp.float32)
            rate = jnp.stack([rates[spread(side * chunks * modes + m, chunks, modes), :] for m in range(modes)])
            target[0] += state * jnp.exp(-rate * back)
            target[1] += state * jnp.exp(-rate * float(slot_total * rows)) * oldest
            return carry

        lax.fori_loop(0, slots, one_slot, 0)

    history_part(partner, part_send)
    part_copy = pltpu.make_async_remote_copy(
        src_ref=part_send,
        dst_ref=part_recv,
        send_sem=part_sem.at[0],
        recv_sem=part_sem.at[1],
        device_id={"seq": partner},
        device_id_type=MESH,
    )
    part_copy.start()
    history_part(q, part_own)
    part_copy.wait()
    residue = jnp.stack([residues[spread(q * chunks * modes + m, chunks, modes), :] for m in range(modes)])
    for k in range(2):
        state_keep[k] = residue * (part_own[k] + part_recv[k])

    @pl.when(jnp.logical_not(first_section))
    def _():
        arrive_rows(0)

    make_gated(0)
    start_sends(0)

    @pl.when(first_section)
    def _():
        for c in range(1, spans):
            make_gated(c)

    weight_copy.wait()
    for c in range(spans):
        project(c)

        def drain(step, carry):
            z_copy(c, step, True).wait_send()
            return carry

        lax.fori_loop(1, tensor_n, drain, 0)
        if c + 1 < spans:
            pl.when(first_section)(lambda: start_sends(c + 1))
        finish(c)
        if c + 1 < spans:

            @pl.when(jnp.logical_not(first_section))
            def _():
                arrive_rows(c + 1)
                make_gated(c + 1)
                start_sends(c + 1)

    for c in range(spans):

        def settle_f(step, carry):
            f_copy(c, step, True).wait_send()
            return carry

        def settle_q(step, carry):
            square_copy(c, me, step, True).wait_send()
            return carry

        lax.fori_loop(0, tensor_n, settle_f, 0)
        lax.fori_loop(1, peers, settle_q, 0)

        @pl.when(has_next)
        def _():
            section_copy(c).wait_send()


def local(
    token_ids,
    leading_span_index,
    embed_table,
    norm_gain,
    decay_rates,
    residues,
    history,
    mix_weight,
):
    tensor_n = lax.axis_size("tensor")
    section_n = lax.axis_size("section")
    seq_n = lax.axis_size("seq")
    spans, rows = token_ids.shape
    vocab, width = embed_table.shape
    modes = decay_rates.shape[1]
    slots = history.shape[1]
    depth, half = mix_weight.shape[1:]
    chunks = half // LANES
    peers = tensor_n * seq_n
    padded = (rows + LANES - 1) // LANES * LANES
    dims = (spans, rows, half, width, modes, slots, vocab, tensor_n, section_n, seq_n)
    f32 = jnp.float32
    smem = pl.BlockSpec(memory_space=pltpu.SMEM)
    vmem = pl.BlockSpec(memory_space=pltpu.VMEM)
    hbm = pl.BlockSpec(memory_space=pl.ANY)
    dma = pltpu.SemaphoreType.DMA
    return pl.pallas_call(
        functools.partial(kernel, dims),
        out_shape=jax.ShapeDtypeStruct((1, spans, rows, half), f32),
        in_specs=[smem, smem, vmem, hbm, hbm, hbm, hbm, hbm],
        out_specs=vmem,
        scratch_shapes=[
            pltpu.VMEM((chunks * vocab, LANES), f32),
            pltpu.VMEM((width // LANES * modes, LANES), f32),
            pltpu.VMEM((width // LANES * modes, LANES), f32),
            pltpu.VMEM((slots, width // LANES * rows, LANES), f32),
            pltpu.VMEM((depth, half), jnp.bfloat16),
            pltpu.VMEM((modes, chunks, LANES), f32),
            pltpu.VMEM((2, modes, chunks, LANES), f32),
            pltpu.VMEM((2, modes, chunks, LANES), f32),
            pltpu.VMEM((2, modes, chunks, LANES), f32),
            pltpu.VMEM((2, modes, chunks, LANES), f32),
            pltpu.VMEM((spans, chunks * rows, LANES), f32),
            pltpu.VMEM((spans, chunks * rows, LANES), f32),
            pltpu.VMEM((spans, chunks * rows, LANES), f32),
            pltpu.VMEM((rows, half), f32),
            pltpu.VMEM((spans, peers, 8, padded), f32),
            pltpu.VMEM((spans, peers, rows, half), jnp.bfloat16),
            pltpu.VMEM((spans, chunks * rows, LANES), jnp.bfloat16),
            pltpu.VMEM((spans, chunks * rows, LANES), jnp.bfloat16),
            dma((5,)),
            dma((2,)),
            dma((spans, peers)),
            dma((spans, peers)),
            dma((spans, tensor_n)),
            dma((spans, tensor_n)),
            dma((spans, tensor_n)),
            dma((spans, tensor_n)),
            dma((spans,)),
            dma((spans,)),
        ],
        compiler_params=pltpu.CompilerParams(
            collective_id=0, has_side_effects=True, vmem_limit_bytes=48 * 1024 * 1024
        ),
    )(
        token_ids,
        leading_span_index,
        norm_gain,
        embed_table,
        decay_rates,
        residues,
        history,
        mix_weight,
    )


def solution(mesh):
    placed = (
        P("groups", None),
        P("groups"),
        P(None, "tensor"),
        P("section", "tensor"),
        P("section", None, "tensor"),
        P("section", None, "tensor"),
        P("section", "seq", "groups", "tensor"),
        P("section", None, ("tensor", "seq")),
    )
    return jax.shard_map(
        local,
        mesh=mesh,
        in_specs=placed,
        out_specs=P("section", None, "groups", ("tensor", "seq")),
        check_vma=False,
    )
```

```python
import functools

import jax
import jax.numpy as jnp
from jax import lax
from jax.experimental import pallas as pl
from jax.experimental.pallas import tpu as pltpu
from jax.sharding import PartitionSpec as P

epsilon = 1e-05
LANES = 128
MESH = pl.DeviceIdType.MESH


def spread(start, count, stride):
    return pl.ds(start, count, stride=stride) if count > 1 else pl.ds(start, 1)


def kernel(
    dims,
    ids_ref,
    lead_ref,
    gain_ref,
    embed_hbm,
    rates_hbm,
    residues_hbm,
    history_hbm,
    weight_hbm,
    out_ref,
    embed,
    rates,
    residues,
    history,
    weight,
    decay,
    part_send,
    part_recv,
    part_own,
    state_keep,
    x_ref,
    normed,
    conv,
    total,
    squares,
    gathered,
    x_send,
    x_recv,
    load_sem,
    part_sem,
    sq_send,
    sq_recv,
    z_send,
    z_recv,
    f_send,
    f_recv,
    s_send,
    s_recv,
):
    spans, parts, span_rows, half, width, modes, slots, vocab, tensor_n, section_n, seq_n = dims
    steps = spans * parts
    rows = span_rows // parts
    chunks = half // LANES
    padded = (rows + LANES - 1) // LANES * LANES
    t = lax.axis_index("tensor")
    s = lax.axis_index("section")
    q = lax.axis_index("seq")
    partner = 1 - q
    me = t * seq_n + q
    peers = tensor_n * seq_n
    model_width = half * peers
    direction = 1 - 2 * ((2 * t) // tensor_n)
    first_section = s == 0
    has_next = s + 1 < section_n

    def at_tensor(step):
        return lax.rem(t + direction * step + tensor_n, tensor_n)

    def loads():
        found = []
        for j in range(width // LANES):
            lanes = pl.ds(j * LANES, LANES)
            found.append((rates_hbm.at[0, :, lanes], rates.at[pl.ds(j * modes, modes), :], 0))
            found.append((residues_hbm.at[0, :, lanes], residues.at[pl.ds(j * modes, modes), :], 1))
            for i in range(slots):
                found.append((history_hbm.at[0, i, :, lanes], history.at[i, pl.ds(j * span_rows, span_rows), :], 2))
        return found

    barrier = pltpu.get_barrier_semaphore()

    def greet(step, carry):
        other = lax.rem(me + step, peers)
        pl.semaphore_signal(
            barrier, inc=1, device_id={"tensor": other // seq_n, "seq": other % seq_n}, device_id_type=MESH
        )
        return carry

    @pl.when(first_section)
    def _():
        for j in range(chunks):
            lanes = pl.ds(pl.multiple_of(q * half + j * LANES, LANES), LANES)
            pltpu.make_async_copy(embed_hbm.at[:, lanes], embed.at[pl.ds(j * vocab, vocab), :], load_sem.at[3]).start()

    for source, target, which in loads():
        pltpu.make_async_copy(source, target, load_sem.at[which]).start()
    weight_copy = pltpu.make_async_copy(weight_hbm.at[0], weight, load_sem.at[4])
    weight_copy.start()

    lax.fori_loop(1, peers, greet, 0)

    @pl.when(has_next)
    def _():
        pl.semaphore_signal(barrier, inc=1, device_id={"section": s + 1}, device_id_type=MESH)

    @pl.when(s > 0)
    def _():
        pl.semaphore_signal(barrier, inc=1, device_id={"section": s - 1}, device_id_type=MESH)

    neighbours = jnp.where(has_next, 1, 0) + jnp.where(s > 0, 1, 0)
    pl.semaphore_wait(barrier, peers - 1 + neighbours)

    def square_copy(c, source, step, send_to):
        other = lax.rem(me + step, peers)
        slot = me if send_to else other
        return pltpu.make_async_remote_copy(
            src_ref=squares.at[c, slot],
            dst_ref=squares.at[c, slot],
            send_sem=sq_send.at[c, step],
            recv_sem=sq_recv.at[c, slot],
            device_id={"tensor": other // seq_n, "seq": other % seq_n},
            device_id_type=MESH,
        )

    def share_squares(c):
        acc = jnp.zeros((rows, LANES), jnp.float32)
        for j in range(chunks):
            piece = x_ref[c, pl.ds(j * rows, rows), :]
            acc = acc + piece * piece
        if padded > rows:
            acc = jnp.concatenate([acc, jnp.zeros((padded - rows, LANES), jnp.float32)], axis=0)
        by_row = jnp.sum(acc.T, axis=0, keepdims=True)
        squares[c, me] = jnp.broadcast_to(by_row, (8, padded))

        def send(step, carry):
            square_copy(c, me, step, True).start()
            return carry

        lax.fori_loop(1, peers, send, 0)

    def embed_rows(c):
        def one(p, carry):
            x_ref[c, spread(p, chunks, rows), :] = embed[
                spread(ids_ref[c // parts, c % parts * rows + p], chunks, vocab), :
            ]
            return carry

        lax.fori_loop(0, rows, one, 0, unroll=8)
        share_squares(c)

    def arrive_rows(c):
        pltpu.make_async_remote_copy(
            src_ref=x_send.at[c],
            dst_ref=x_recv.at[c],
            send_sem=s_send.at[c],
            recv_sem=s_recv.at[c],
            device_id={"section": s - 1},
            device_id_type=MESH,
        ).wait_recv()
        for j in range(chunks):
            block = pl.ds(j * rows, rows)
            x_ref[c, block, :] = x_recv[c, block, :].astype(jnp.float32)
        share_squares(c)

    def z_copy(c, step, send_to):
        other = at_tensor(step)
        slot = me if send_to else other * seq_n + q
        return pltpu.make_async_remote_copy(
            src_ref=gathered.at[c, slot],
            dst_ref=gathered.at[c, slot],
            send_sem=z_send.at[c, other],
            recv_sem=z_recv.at[c, t if send_to else other],
            device_id={"tensor": other},
            device_id_type=MESH,
        )

    def f_copy(c, step, send_to):
        other = at_tensor(step)
        slot = other * seq_n + (q if send_to else partner)
        return pltpu.make_async_remote_copy(
            src_ref=gathered.at[c, slot],
            dst_ref=gathered.at[c, slot],
            send_sem=f_send.at[c, other],
            recv_sem=f_recv.at[c, other],
            device_id={"seq": partner},
            device_id_type=MESH,
        )

    def start_sends(c):
        f_copy(c, 0, True).start()

        def send(step, carry):
            z_copy(c, step, True).start()
            return carry

        lax.fori_loop(1, tensor_n, send, 0)

    def make_gated(c):
        def wait(step, carry):
            square_copy(c, me, step, False).wait_recv()
            return carry

        lax.fori_loop(1, peers, wait, 0)
        summed = jnp.sum(squares[c], axis=0)
        scale = lax.rsqrt(summed * (1.0 / model_width) + epsilon)
        scale = jnp.broadcast_to(scale[0:1, :], (LANES, padded)).T[:rows]
        for j in range(chunks):
            block = pl.ds(j * rows, rows)
            gain = gain_ref[0:1, pl.ds(pl.multiple_of(q * half + j * LANES, LANES), LANES)]
            normed[c, block, :] = x_ref[c, block, :] * (scale * gain)

        decays = decay[...]
        gains = jnp.stack([residues[spread(q * chunks * modes + m, chunks, modes), :] for m in range(modes)])

        def step(p, state):
            row = normed[c, spread(p, chunks, rows), :]
            state = state * decays + gains * row[None]
            conv[c, spread(p, chunks, rows), :] = jnp.sum(state, axis=0)
            return state

        state = lax.fori_loop(0, rows, step, state_keep[0], unroll=4)
        state_keep[0] = state - state_keep[1] if c % parts == parts - 1 else state
        for j in range(chunks):
            block = pl.ds(j * rows, rows)
            gathered[c, me, :, pl.ds(j * LANES, LANES)] = (normed[c, block, :] * conv[c, block, :]).astype(
                jnp.bfloat16
            )

    def multiply(c, slot):
        block = weight[pl.ds(pl.multiple_of(slot * half, half), half), :]
        total[...] += jnp.dot(gathered[c, slot], block, preferred_element_type=jnp.float32)

    def project(c):
        own = weight[pl.ds(pl.multiple_of(me * half, half), half), :]
        total[...] = jnp.dot(gathered[c, me], own, preferred_element_type=jnp.float32)

        def take(step, carry):
            z_copy(c, step, False).wait_recv()
            f_copy(c, step, True).start()
            multiply(c, at_tensor(step) * seq_n + q)
            f_copy(c, step - 1, False).wait_recv()
            multiply(c, at_tensor(step - 1) * seq_n + partner)
            return carry

        lax.fori_loop(1, tensor_n, take, 0)

    def finish(c):
        f_copy(c, tensor_n - 1, False).wait_recv()
        multiply(c, at_tensor(tensor_n - 1) * seq_n + partner)
        for j in range(chunks):
            lanes = pl.ds(j * LANES, LANES)
            block = pl.ds(j * rows, rows)
            value = x_ref[c, block, :] + total[:, lanes]
            out_ref[0, c // parts, pl.ds(c % parts * rows, rows), lanes] = value
            x_send[c, block, :] = value.astype(jnp.bfloat16)

        @pl.when(has_next)
        def _():
            section_copy(c).start()

    def section_copy(c):
        return pltpu.make_async_remote_copy(
            src_ref=x_send.at[c],
            dst_ref=x_recv.at[c],
            send_sem=s_send.at[c],
            recv_sem=s_recv.at[c],
            device_id={"section": s + 1},
            device_id_type=MESH,
        )

    @pl.when(first_section)
    def _():
        pltpu.make_async_copy(embed, embed, load_sem.at[3]).wait()
        for c in range(steps):
            embed_rows(c)

    pltpu.make_async_copy(rates, rates, load_sem.at[0]).wait()
    pltpu.make_async_copy(residues, residues, load_sem.at[1]).wait()
    pltpu.make_async_copy(history, history, load_sem.at[2]).wait()
    first_span = lead_ref[0]
    slot_total = slots * seq_n

    def history_part(side, target):
        rate = jnp.stack([rates[spread(side * chunks * modes + m, chunks, modes), :] for m in range(modes)])
        decay[...] = jnp.exp(-rate)
        target[...] = jnp.zeros_like(target)

        def one_slot(i, carry):
            decays = decay[...]

            def step(l, state):
                row = history[i, spread(side * chunks * span_rows + l, chunks, span_rows), :]
                return state * decays + row[None]

            state = lax.fori_loop(0, span_rows, step, jnp.zeros((modes, chunks, LANES), jnp.float32), unroll=8)
            age = lax.rem(first_span - 1 - (q * slots + i), slot_total) + 1
            back = ((age - 1) * span_rows).astype(jnp.float32)
            oldest = jnp.where(age == slot_total, 1.0, 0.0).astype(jnp.float32)
            rate = jnp.stack([rates[spread(side * chunks * modes + m, chunks, modes), :] for m in range(modes)])
            target[0] += state * jnp.exp(-rate * back)
            target[1] += state * jnp.exp(-rate * float(slot_total * span_rows)) * oldest
            return carry

        lax.fori_loop(0, slots, one_slot, 0)

    history_part(partner, part_send)
    part_copy = pltpu.make_async_remote_copy(
        src_ref=part_send,
        dst_ref=part_recv,
        send_sem=part_sem.at[0],
        recv_sem=part_sem.at[1],
        device_id={"seq": partner},
        device_id_type=MESH,
    )
    part_copy.start()
    history_part(q, part_own)
    part_copy.wait()
    residue = jnp.stack([residues[spread(q * chunks * modes + m, chunks, modes), :] for m in range(modes)])
    for k in range(2):
        state_keep[k] = residue * (part_own[k] + part_recv[k])

    @pl.when(jnp.logical_not(first_section))
    def _():
        arrive_rows(0)

    make_gated(0)
    start_sends(0)

    weight_copy.wait()
    for c in range(steps):
        if c + 1 < steps:

            @pl.when(first_section)
            def _():
                make_gated(c + 1)
                start_sends(c + 1)

        project(c)
        finish(c)
        if c + 1 < steps:

            @pl.when(jnp.logical_not(first_section))
            def _():
                arrive_rows(c + 1)
                make_gated(c + 1)
                start_sends(c + 1)

    for c in range(steps):

        def settle_z(step, carry):
            z_copy(c, step, True).wait_send()
            return carry

        lax.fori_loop(1, tensor_n, settle_z, 0)

        def settle_f(step, carry):
            f_copy(c, step, True).wait_send()
            return carry

        def settle_q(step, carry):
            square_copy(c, me, step, True).wait_send()
            return carry

        lax.fori_loop(0, tensor_n, settle_f, 0)
        lax.fori_loop(1, peers, settle_q, 0)

        @pl.when(has_next)
        def _():
            section_copy(c).wait_send()


def local(
    token_ids,
    leading_span_index,
    embed_table,
    norm_gain,
    decay_rates,
    residues,
    history,
    mix_weight,
):
    tensor_n = lax.axis_size("tensor")
    section_n = lax.axis_size("section")
    seq_n = lax.axis_size("seq")
    spans, rows = token_ids.shape
    vocab, width = embed_table.shape
    modes = decay_rates.shape[1]
    slots = history.shape[1]
    depth, half = mix_weight.shape[1:]
    chunks = half // LANES
    peers = tensor_n * seq_n
    parts = 2 if rows % 32 == 0 else 1
    steps = spans * parts
    part_rows = rows // parts
    padded = (part_rows + LANES - 1) // LANES * LANES
    dims = (spans, parts, rows, half, width, modes, slots, vocab, tensor_n, section_n, seq_n)
    f32 = jnp.float32
    smem = pl.BlockSpec(memory_space=pltpu.SMEM)
    vmem = pl.BlockSpec(memory_space=pltpu.VMEM)
    hbm = pl.BlockSpec(memory_space=pl.ANY)
    dma = pltpu.SemaphoreType.DMA
    return pl.pallas_call(
        functools.partial(kernel, dims),
        out_shape=jax.ShapeDtypeStruct((1, spans, rows, half), f32),
        in_specs=[smem, smem, vmem, hbm, hbm, hbm, hbm, hbm],
        out_specs=vmem,
        scratch_shapes=[
            pltpu.VMEM((chunks * vocab, LANES), f32),
            pltpu.VMEM((width // LANES * modes, LANES), f32),
            pltpu.VMEM((width // LANES * modes, LANES), f32),
            pltpu.VMEM((slots, width // LANES * rows, LANES), f32),
            pltpu.VMEM((depth, half), jnp.bfloat16),
            pltpu.VMEM((modes, chunks, LANES), f32),
            pltpu.VMEM((2, modes, chunks, LANES), f32),
            pltpu.VMEM((2, modes, chunks, LANES), f32),
            pltpu.VMEM((2, modes, chunks, LANES), f32),
            pltpu.VMEM((2, modes, chunks, LANES), f32),
            pltpu.VMEM((steps, chunks * part_rows, LANES), f32),
            pltpu.VMEM((steps, chunks * part_rows, LANES), f32),
            pltpu.VMEM((steps, chunks * part_rows, LANES), f32),
            pltpu.VMEM((part_rows, half), f32),
            pltpu.VMEM((steps, peers, 8, padded), f32),
            pltpu.VMEM((steps, peers, part_rows, half), jnp.bfloat16),
            pltpu.VMEM((steps, chunks * part_rows, LANES), jnp.bfloat16),
            pltpu.VMEM((steps, chunks * part_rows, LANES), jnp.bfloat16),
            dma((5,)),
            dma((2,)),
            dma((steps, peers)),
            dma((steps, peers)),
            dma((steps, tensor_n)),
            dma((steps, tensor_n)),
            dma((steps, tensor_n)),
            dma((steps, tensor_n)),
            dma((steps,)),
            dma((steps,)),
        ],
        compiler_params=pltpu.CompilerParams(
            collective_id=0, has_side_effects=True, vmem_limit_bytes=60 * 1024 * 1024
        ),
    )(
        token_ids,
        leading_span_index,
        norm_gain,
        embed_table,
        decay_rates,
        residues,
        history,
        mix_weight,
    )


def solution(mesh):
    placed = (
        P("groups", None),
        P("groups"),
        P(None, "tensor"),
        P("section", "tensor"),
        P("section", None, "tensor"),
        P("section", None, "tensor"),
        P("section", "seq", "groups", "tensor"),
        P("section", None, ("tensor", "seq")),
    )
    return jax.shard_map(
        local,
        mesh=mesh,
        in_specs=placed,
        out_specs=P("section", None, "groups", ("tensor", "seq")),
        check_vma=False,
    )
```

```python
import functools

import jax
import jax.numpy as jnp
from jax import lax
from jax.experimental import pallas as pl
from jax.experimental.pallas import tpu as pltpu
from jax.sharding import PartitionSpec as P

epsilon = 1e-05
LANES = 128
MESH = pl.DeviceIdType.MESH


def spread(start, count, stride):
    return pl.ds(start, count, stride=stride) if count > 1 else pl.ds(start, 1)


def kernel(
    dims,
    ids_ref,
    lead_ref,
    gain_ref,
    embed_hbm,
    rates_hbm,
    residues_hbm,
    history_hbm,
    weight_hbm,
    out_ref,
    embed,
    rates,
    residues,
    history,
    weight,
    decay,
    part_send,
    part_recv,
    part_own,
    state_keep,
    x_ref,
    normed,
    conv,
    total,
    squares,
    gathered,
    x_send,
    x_recv,
    load_sem,
    part_sem,
    sq_send,
    sq_recv,
    z_send,
    z_recv,
    f_send,
    f_recv,
    s_send,
    s_recv,
):
    spans, parts, span_rows, half, width, modes, slots, vocab, tensor_n, section_n, seq_n = dims
    steps = spans * parts
    rows = span_rows // parts
    chunks = half // LANES
    padded = (rows + LANES - 1) // LANES * LANES
    t = lax.axis_index("tensor")
    s = lax.axis_index("section")
    q = lax.axis_index("seq")
    partner = 1 - q
    me = t * seq_n + q
    peers = tensor_n * seq_n
    model_width = half * peers
    direction = 1 - 2 * ((2 * t) // tensor_n)
    first_section = s == 0
    has_next = s + 1 < section_n

    def at_tensor(step):
        return lax.rem(t + direction * step + tensor_n, tensor_n)

    def loads():
        found = []
        for j in range(width // LANES):
            lanes = pl.ds(j * LANES, LANES)
            found.append((rates_hbm.at[0, :, lanes], rates.at[pl.ds(j * modes, modes), :], 0))
            found.append((residues_hbm.at[0, :, lanes], residues.at[pl.ds(j * modes, modes), :], 1))
            for i in range(slots):
                found.append((history_hbm.at[0, i, :, lanes], history.at[i, pl.ds(j * span_rows, span_rows), :], 2))
        return found

    barrier = pltpu.get_barrier_semaphore()

    def greet(step, carry):
        other = lax.rem(me + step, peers)
        pl.semaphore_signal(
            barrier, inc=1, device_id={"tensor": other // seq_n, "seq": other % seq_n}, device_id_type=MESH
        )
        return carry

    @pl.when(first_section)
    def _():
        for j in range(chunks):
            lanes = pl.ds(pl.multiple_of(q * half + j * LANES, LANES), LANES)
            pltpu.make_async_copy(embed_hbm.at[:, lanes], embed.at[pl.ds(j * vocab, vocab), :], load_sem.at[3]).start()

    for source, target, which in loads():
        pltpu.make_async_copy(source, target, load_sem.at[which]).start()
    weight_copy = pltpu.make_async_copy(weight_hbm.at[0], weight, load_sem.at[4])
    weight_copy.start()

    lax.fori_loop(1, peers, greet, 0)

    @pl.when(has_next)
    def _():
        pl.semaphore_signal(barrier, inc=1, device_id={"section": s + 1}, device_id_type=MESH)

    @pl.when(s > 0)
    def _():
        pl.semaphore_signal(barrier, inc=1, device_id={"section": s - 1}, device_id_type=MESH)

    neighbours = jnp.where(has_next, 1, 0) + jnp.where(s > 0, 1, 0)
    pl.semaphore_wait(barrier, peers - 1 + neighbours)

    def square_copy(c, source, step, send_to):
        other = lax.rem(me + step, peers)
        slot = me if send_to else other
        return pltpu.make_async_remote_copy(
            src_ref=squares.at[c, slot],
            dst_ref=squares.at[c, slot],
            send_sem=sq_send.at[c, step],
            recv_sem=sq_recv.at[c, slot],
            device_id={"tensor": other // seq_n, "seq": other % seq_n},
            device_id_type=MESH,
        )

    def share_squares(c):
        acc = jnp.zeros((rows, LANES), jnp.float32)
        for j in range(chunks):
            piece = x_ref[c, pl.ds(j * rows, rows), :]
            acc = acc + piece * piece
        if padded > rows:
            acc = jnp.concatenate([acc, jnp.zeros((padded - rows, LANES), jnp.float32)], axis=0)
        by_row = jnp.sum(acc.T, axis=0, keepdims=True)
        squares[c, me] = jnp.broadcast_to(by_row, (8, padded))

        def send(step, carry):
            square_copy(c, me, step, True).start()
            return carry

        lax.fori_loop(1, peers, send, 0)

    def embed_rows(c):
        def one(p, carry):
            x_ref[c, spread(p, chunks, rows), :] = embed[
                spread(ids_ref[c // parts, c % parts * rows + p], chunks, vocab), :
            ]
            return carry

        lax.fori_loop(0, rows, one, 0, unroll=8)
        share_squares(c)

    def arrive_rows(c):
        pltpu.make_async_remote_copy(
            src_ref=x_send.at[c],
            dst_ref=x_recv.at[c],
            send_sem=s_send.at[c],
            recv_sem=s_recv.at[c],
            device_id={"section": s - 1},
            device_id_type=MESH,
        ).wait_recv()
        for j in range(chunks):
            block = pl.ds(j * rows, rows)
            x_ref[c, block, :] = x_recv[c, block, :].astype(jnp.float32)
        share_squares(c)

    def z_copy(c, step, send_to):
        other = at_tensor(step)
        slot = me if send_to else other * seq_n + q
        return pltpu.make_async_remote_copy(
            src_ref=gathered.at[c, slot],
            dst_ref=gathered.at[c, slot],
            send_sem=z_send.at[c, other],
            recv_sem=z_recv.at[c, t if send_to else other],
            device_id={"tensor": other},
            device_id_type=MESH,
        )

    def f_copy(c, step, send_to):
        other = at_tensor(step)
        slot = other * seq_n + (q if send_to else partner)
        return pltpu.make_async_remote_copy(
            src_ref=gathered.at[c, slot],
            dst_ref=gathered.at[c, slot],
            send_sem=f_send.at[c, other],
            recv_sem=f_recv.at[c, other],
            device_id={"seq": partner},
            device_id_type=MESH,
        )

    def start_sends(c):
        f_copy(c, 0, True).start()

        def send(step, carry):
            z_copy(c, step, True).start()
            return carry

        lax.fori_loop(1, tensor_n, send, 0)

    def make_gated(c):
        def wait(step, carry):
            square_copy(c, me, step, False).wait_recv()
            return carry

        lax.fori_loop(1, peers, wait, 0)
        summed = jnp.sum(squares[c], axis=0)
        scale = lax.rsqrt(summed * (1.0 / model_width) + epsilon)
        scale = jnp.broadcast_to(scale[0:1, :], (LANES, padded)).T[:rows]
        for j in range(chunks):
            block = pl.ds(j * rows, rows)
            gain = gain_ref[0:1, pl.ds(pl.multiple_of(q * half + j * LANES, LANES), LANES)]
            normed[c, block, :] = x_ref[c, block, :] * (scale * gain)

        decays = decay[...]
        gains = jnp.stack([residues[spread(q * chunks * modes + m, chunks, modes), :] for m in range(modes)])

        def step(p, state):
            row = normed[c, spread(p, chunks, rows), :]
            state = state * decays + gains * row[None]
            conv[c, spread(p, chunks, rows), :] = jnp.sum(state, axis=0)
            return state

        state = lax.fori_loop(0, rows, step, state_keep[0], unroll=4)
        state_keep[0] = state - state_keep[1] if c % parts == parts - 1 else state
        for j in range(chunks):
            block = pl.ds(j * rows, rows)
            gathered[c, me, :, pl.ds(j * LANES, LANES)] = (normed[c, block, :] * conv[c, block, :]).astype(
                jnp.bfloat16
            )

    def multiply(c, slot):
        block = weight[pl.ds(pl.multiple_of(slot * half, half), half), :]
        total[...] += jnp.dot(gathered[c, slot], block, preferred_element_type=jnp.float32)

    def project(c):
        own = weight[pl.ds(pl.multiple_of(me * half, half), half), :]
        total[...] = jnp.dot(gathered[c, me], own, preferred_element_type=jnp.float32)

        def take(step, carry):
            z_copy(c, step, False).wait_recv()
            f_copy(c, step, True).start()
            multiply(c, at_tensor(step) * seq_n + q)
            f_copy(c, step - 1, False).wait_recv()
            multiply(c, at_tensor(step - 1) * seq_n + partner)
            return carry

        lax.fori_loop(1, tensor_n, take, 0)

    def finish(c):
        f_copy(c, tensor_n - 1, False).wait_recv()
        multiply(c, at_tensor(tensor_n - 1) * seq_n + partner)
        for j in range(chunks):
            lanes = pl.ds(j * LANES, LANES)
            block = pl.ds(j * rows, rows)
            value = x_ref[c, block, :] + total[:, lanes]
            out_ref[0, c // parts, pl.ds(c % parts * rows, rows), lanes] = value
            x_send[c, block, :] = value.astype(jnp.bfloat16)

        @pl.when(has_next)
        def _():
            section_copy(c).start()

    def section_copy(c):
        return pltpu.make_async_remote_copy(
            src_ref=x_send.at[c],
            dst_ref=x_recv.at[c],
            send_sem=s_send.at[c],
            recv_sem=s_recv.at[c],
            device_id={"section": s + 1},
            device_id_type=MESH,
        )

    @pl.when(first_section)
    def _():
        pltpu.make_async_copy(embed, embed, load_sem.at[3]).wait()
        for c in range(steps):
            embed_rows(c)

    pltpu.make_async_copy(rates, rates, load_sem.at[0]).wait()
    pltpu.make_async_copy(residues, residues, load_sem.at[1]).wait()
    pltpu.make_async_copy(history, history, load_sem.at[2]).wait()
    first_span = lead_ref[0]
    slot_total = slots * seq_n

    def history_part(side, target):
        rate = jnp.stack([rates[spread(side * chunks * modes + m, chunks, modes), :] for m in range(modes)])
        decay[...] = jnp.exp(-rate)
        target[...] = jnp.zeros_like(target)

        def one_slot(i, carry):
            decays = decay[...]

            def step(l, state):
                row = history[i, spread(side * chunks * span_rows + l, chunks, span_rows), :]
                return state * decays + row[None]

            state = lax.fori_loop(0, span_rows, step, jnp.zeros((modes, chunks, LANES), jnp.float32), unroll=8)
            age = lax.rem(first_span - 1 - (q * slots + i), slot_total) + 1
            back = ((age - 1) * span_rows).astype(jnp.float32)
            oldest = jnp.where(age == slot_total, 1.0, 0.0).astype(jnp.float32)
            rate = jnp.stack([rates[spread(side * chunks * modes + m, chunks, modes), :] for m in range(modes)])
            target[0] += state * jnp.exp(-rate * back)
            target[1] += state * jnp.exp(-rate * float(slot_total * span_rows)) * oldest
            return carry

        lax.fori_loop(0, slots, one_slot, 0)

    history_part(partner, part_send)
    part_copy = pltpu.make_async_remote_copy(
        src_ref=part_send,
        dst_ref=part_recv,
        send_sem=part_sem.at[0],
        recv_sem=part_sem.at[1],
        device_id={"seq": partner},
        device_id_type=MESH,
    )
    part_copy.start()
    history_part(q, part_own)
    part_copy.wait()
    residue = jnp.stack([residues[spread(q * chunks * modes + m, chunks, modes), :] for m in range(modes)])
    for k in range(2):
        state_keep[k] = residue * (part_own[k] + part_recv[k])

    @pl.when(jnp.logical_not(first_section))
    def _():
        arrive_rows(0)

    make_gated(0)
    start_sends(0)

    weight_copy.wait()
    for c in range(steps):
        if c + 1 < steps:

            @pl.when(jnp.logical_not(first_section))
            def _():
                arrive_rows(c + 1)

            make_gated(c + 1)
            start_sends(c + 1)

        project(c)
        finish(c)

    for c in range(steps):

        def settle_z(step, carry):
            z_copy(c, step, True).wait_send()
            return carry

        lax.fori_loop(1, tensor_n, settle_z, 0)

        def settle_f(step, carry):
            f_copy(c, step, True).wait_send()
            return carry

        def settle_q(step, carry):
            square_copy(c, me, step, True).wait_send()
            return carry

        lax.fori_loop(0, tensor_n, settle_f, 0)
        lax.fori_loop(1, peers, settle_q, 0)

        @pl.when(has_next)
        def _():
            section_copy(c).wait_send()


def local(
    token_ids,
    leading_span_index,
    embed_table,
    norm_gain,
    decay_rates,
    residues,
    history,
    mix_weight,
):
    tensor_n = lax.axis_size("tensor")
    section_n = lax.axis_size("section")
    seq_n = lax.axis_size("seq")
    spans, rows = token_ids.shape
    vocab, width = embed_table.shape
    modes = decay_rates.shape[1]
    slots = history.shape[1]
    depth, half = mix_weight.shape[1:]
    chunks = half // LANES
    peers = tensor_n * seq_n
    parts = 2 if rows % 32 == 0 else 1
    steps = spans * parts
    part_rows = rows // parts
    padded = (part_rows + LANES - 1) // LANES * LANES
    dims = (spans, parts, rows, half, width, modes, slots, vocab, tensor_n, section_n, seq_n)
    f32 = jnp.float32
    smem = pl.BlockSpec(memory_space=pltpu.SMEM)
    vmem = pl.BlockSpec(memory_space=pltpu.VMEM)
    hbm = pl.BlockSpec(memory_space=pl.ANY)
    dma = pltpu.SemaphoreType.DMA
    return pl.pallas_call(
        functools.partial(kernel, dims),
        out_shape=jax.ShapeDtypeStruct((1, spans, rows, half), f32),
        in_specs=[smem, smem, vmem, hbm, hbm, hbm, hbm, hbm],
        out_specs=vmem,
        scratch_shapes=[
            pltpu.VMEM((chunks * vocab, LANES), f32),
            pltpu.VMEM((width // LANES * modes, LANES), f32),
            pltpu.VMEM((width // LANES * modes, LANES), f32),
            pltpu.VMEM((slots, width // LANES * rows, LANES), f32),
            pltpu.VMEM((depth, half), jnp.bfloat16),
            pltpu.VMEM((modes, chunks, LANES), f32),
            pltpu.VMEM((2, modes, chunks, LANES), f32),
            pltpu.VMEM((2, modes, chunks, LANES), f32),
            pltpu.VMEM((2, modes, chunks, LANES), f32),
            pltpu.VMEM((2, modes, chunks, LANES), f32),
            pltpu.VMEM((steps, chunks * part_rows, LANES), f32),
            pltpu.VMEM((steps, chunks * part_rows, LANES), f32),
            pltpu.VMEM((steps, chunks * part_rows, LANES), f32),
            pltpu.VMEM((part_rows, half), f32),
            pltpu.VMEM((steps, peers, 8, padded), f32),
            pltpu.VMEM((steps, peers, part_rows, half), jnp.bfloat16),
            pltpu.VMEM((steps, chunks * part_rows, LANES), jnp.bfloat16),
            pltpu.VMEM((steps, chunks * part_rows, LANES), jnp.bfloat16),
            dma((5,)),
            dma((2,)),
            dma((steps, peers)),
            dma((steps, peers)),
            dma((steps, tensor_n)),
            dma((steps, tensor_n)),
            dma((steps, tensor_n)),
            dma((steps, tensor_n)),
            dma((steps,)),
            dma((steps,)),
        ],
        compiler_params=pltpu.CompilerParams(
            collective_id=0, has_side_effects=True, vmem_limit_bytes=60 * 1024 * 1024
        ),
    )(
        token_ids,
        leading_span_index,
        norm_gain,
        embed_table,
        decay_rates,
        residues,
        history,
        mix_weight,
    )


def solution(mesh):
    placed = (
        P("groups", None),
        P("groups"),
        P(None, "tensor"),
        P("section", "tensor"),
        P("section", None, "tensor"),
        P("section", None, "tensor"),
        P("section", "seq", "groups", "tensor"),
        P("section", None, ("tensor", "seq")),
    )
    return jax.shard_map(
        local,
        mesh=mesh,
        in_specs=placed,
        out_specs=P("section", None, "groups", ("tensor", "seq")),
        check_vma=False,
    )
```
